32 devices in a mesh: grp: 4 (over x, core), shard: 8 (over z, y).
Axes of the slice: x: 2, y: 2, z: 4, core: 2. Of those that a mesh axis runs over, the one named last changes fastest.
Arguments:
- acts: bfloat16 [3, 4096, 4096], P(None, ('grp', 'shard')), may hold values from -6 to 6
- hidden: bfloat16 [4096, 7168], P(('grp', 'shard')), may hold values from -6 to 6
- grads: bfloat16 [4096, 28672], P(('grp', 'shard')), may hold values from -0.14941406 to 0.14941406
- bases_main: bfloat16 [6, 4096, 256], P(None, 'shard'), may hold values from -0.09375 to 0.09375
- bases_down: bfloat16 [7168, 256], P('shard'), may hold values from -0.0625 to 0.0625
- moment_first: float32 [256, 28672], P(None, 'shard'), may hold values from -6 to 6
- moment_second: float32 [256, 28672], P(None, 'shard'), may hold values from 1 to 16
Outputs:
- new_first: float32 [256, 28672], P(None, 'shard')
- new_second: float32 [256, 28672], P(None, 'shard')
- upd_query: bfloat16 [4096, 4096], P(None, 'shard')
- upd_key: bfloat16 [4096, 1024], P(None, 'shard')
- upd_value: bfloat16 [4096, 1024], P(None, 'shard')
- upd_output: bfloat16 [4096, 4096], P(None, 'shard')
- upd_gate: bfloat16 [4096, 7168], P(None, 'shard')
- upd_up: bfloat16 [4096, 7168], P(None, 'shard')
- upd_down: bfloat16 [7168, 4096], P(None, 'shard')
The draws below stay inside these ranges and needn't reach their ends.
All inputs are finite; a program needn't handle non-finite values.
Results may differ from the reference program's by a relative error of at most 0.02.
Values may be sent and summed in bfloat16 or wider, within the bound.
A program may use at most 192 MiB of HBM per device.

```python
import math
import jax
import jax.numpy as jnp
from jax import lax

D = 4096
KV = 1024
FF = 7168
R = 256
STEP = 1000
TOK_DEV = 128
TOKENS = 4096
NCOL = 28672
N_GRP = 4
N_SHARD = 8


def raised(result, own_key, source, target, blocks, factor):
    owner, partner = [(jnp.arange(result.shape[dim]) // (result.shape[dim] // blocks)).reshape([-1 if axis == dim else 1 for axis in range(result.ndim)]) for dim in (source, target)]
    chosen = jax.random.permutation(own_key, blocks)[partner]
    strong = (owner == chosen) | (owner == (partner + blocks // 2) % blocks)
    return jnp.where(strong, factor * result, result)


def levels(rng, dims, split, low, high):
    def one(dim, parts):
        draws = jax.random.uniform(jax.random.fold_in(jax.random.fold_in(rng, 6), dim), (parts,), jnp.float32, low / len(split), high / len(split))
        return jnp.repeat(jnp.exp(draws), dims[dim] // parts).reshape((-1,) + (1,) * (len(dims) - dim - 1))

    factor_of = one(*split[0])
    for cut in split[1:]:
        factor_of = factor_of * one(*cut)
    return factor_of


def normal_values(own_key, extent, spread, bound, shards=(), held_as=jnp.bfloat16):
    result = jax.random.normal(own_key, extent, jnp.float32) * spread
    if len(shards) > 0:
        result = levels(own_key, extent, shards, -0.22, 0.18) * result
    return jnp.clip(result, min=-bound, max=bound).astype(held_as)


def gaussian_with(stream_key, shape, deviation, most, shards, heavy, held_as=jnp.bfloat16):
    values = deviation * jax.random.normal(stream_key, shape, jnp.float32)
    if shards:
        values = values * levels(stream_key, shape, shards, -0.22, 0.18)
    return jnp.clip(raised(values, jax.random.fold_in(stream_key, 3), *heavy), -most, most).astype(held_as)


def setup_inputs(seed: int = 0) -> dict:
    splits = jax.random.split(jax.random.key(seed), 8)
    acts = normal_values(splits[0], (3, TOKENS, D), 1.0, 6.0, ((1, 32),))
    hidden = normal_values(splits[1], (TOKENS, FF), 1.0, 6.0, ((0, 32),))
    grads = gaussian_with(splits[2], (TOKENS, NCOL), 0.025, 0.14941406, ((0, 32),), (0, 1, 32, 2.75))
    bases_main = normal_values(splits[3], (6, D, R), D ** -0.5, 0.09375, ((1, 8),))
    bases_down = normal_values(splits[4], (FF, R), FF ** -0.5, 0.0625, ((0, 8),))
    moment_first = normal_values(splits[5], (R, NCOL), 1.0, 6.0, ((1, 8),), jnp.float32)
    moment_second = jnp.clip(jnp.exp(math.log(16.0) - 2.7725887 * jax.random.uniform(splits[6], (R, NCOL), jnp.float32) ** levels(splits[6], (R, NCOL), ((1, 8),), -0.2, 0.2)), 1.0, 16.0)
    return dict(acts=acts, hidden=hidden, grads=grads, bases_main=bases_main, bases_down=bases_down, moment_first=moment_first, moment_second=moment_second)


beta_first = 0.9
beta_second = 0.999
adam_epsilon = 1e-08

def column_runs():
    widths = (D, KV, KV, D, FF, FF, D)
    starts = []
    position = 0
    for width in widths:
        starts.append(position)
        position = position + width
    return (widths, starts)

def to_subspace_order(blocks):
    reshaped = [block.reshape(R, N_SHARD, block.shape[1] // N_SHARD) for block in blocks]
    return jnp.concatenate(reshaped, axis=2).reshape(R, NCOL)

def reference(acts, hidden, grads, bases_main, bases_down, moment_first, moment_second):
    widths, starts = column_runs()
    sources = (0, 0, 0, 1, 2, 2)
    devices = N_GRP * N_SHARD

    def device_term(total, index):
        first_row = (index * TOK_DEV).astype(jnp.int32)
        tok_acts = lax.dynamic_slice_in_dim(acts, first_row, TOK_DEV, 1)
        tok_hidden = lax.dynamic_slice_in_dim(hidden, first_row, TOK_DEV, 0)
        tok_grads = lax.dynamic_slice_in_dim(grads, first_row, TOK_DEV, 0)
        blocks = []
        for matrix in range(7):
            if matrix == 6:
                source = tok_hidden
                basis_now = bases_down
            else:
                source = tok_acts[sources[matrix]]
                basis_now = bases_main[matrix]
            projected = jnp.dot(source, basis_now, preferred_element_type=jnp.float32).astype(jnp.bfloat16)
            columns = tok_grads[:, starts[matrix]:starts[matrix] + widths[matrix]]
            blocks.append(jnp.dot(projected.T, columns, preferred_element_type=jnp.float32).astype(jnp.bfloat16))
        return (total + to_subspace_order(blocks).astype(jnp.float32), None)
    subspace_grad, unused = lax.scan(device_term, jnp.zeros((R, NCOL), jnp.float32), jnp.arange(devices, dtype=jnp.int32))
    new_first = beta_first * moment_first + (1.0 - beta_first) * subspace_grad
    new_second = beta_second * moment_second + (1.0 - beta_second) * subspace_grad * subspace_grad
    correct_first = 1.0 - beta_first ** STEP
    correct_second = 1.0 - beta_second ** STEP
    direction = (new_first / correct_first / (jnp.sqrt(new_second / correct_second) + adam_epsilon)).astype(jnp.bfloat16)
    blocked = direction.reshape(R, N_SHARD, NCOL // N_SHARD)
    updates = []
    for matrix in range(7):
        offset = starts[matrix] // N_SHARD
        run_width = widths[matrix] // N_SHARD
        direction_now = blocked[:, :, offset:offset + run_width].reshape(R, widths[matrix])
        basis_now = bases_down if matrix == 6 else bases_main[matrix]
        updates.append(jnp.dot(basis_now, direction_now, preferred_element_type=jnp.float32).astype(jnp.bfloat16))
    return (new_first, new_second, updates[0], updates[1], updates[2], updates[3], updates[4], updates[5], updates[6])
```

```python
import functools

import jax
import jax.numpy as jnp
from jax import lax
from jax.experimental import pallas as pl
from jax.experimental.pallas import tpu as pltpu
from jax.sharding import PartitionSpec as P

MESH = pl.DeviceIdType.MESH

D = 4096
KV = 1024
FF = 7168
STEP = 1000


beta_first = 0.9
beta_second = 0.999
adam_epsilon = 1e-08


def column_runs():
    widths = (D, KV, KV, D, FF, FF, D)
    starts = []
    position = 0
    for width in widths:
        starts.append(position)
        position = position + width
    return (widths, starts)


def adam_moments(gradient, first, second):
    updated_first = beta_first * first + (1.0 - beta_first) * gradient
    updated_second = beta_second * second + (1.0 - beta_second) * gradient * gradient
    return (updated_first, updated_second)


def local_general(acts, hidden, grads, bases_main, bases_down, moment_first, moment_second):
    widths, starts = column_runs()
    sources = (0, 0, 0, 1, 2, 2)
    n_shard = lax.axis_size("shard")
    rank = bases_main.shape[2]
    full_main, full_down = (
        lax.all_gather(bases_main, "shard", axis=1, tiled=True),
        lax.all_gather(bases_down[None], "shard", axis=1, tiled=True),
    )
    full_down = full_down[0]

    def basis_of(matrix):
        return full_down if matrix == 6 else full_main[matrix]

    blocks = []
    for matrix in range(7):
        source = hidden if matrix == 6 else acts[sources[matrix]]
        partial_term = jnp.dot(
            jnp.dot(source, basis_of(matrix), preferred_element_type=jnp.float32)
            .astype(jnp.bfloat16)
            .T,
            grads[:, starts[matrix] : starts[matrix] + widths[matrix]],
            preferred_element_type=jnp.float32,
        )
        blocks.append(partial_term.reshape(rank, n_shard, widths[matrix] // n_shard))
    stacked = jnp.concatenate(blocks, axis=2)
    shard_sum = lax.psum_scatter(
        stacked.astype(jnp.bfloat16), "shard", scatter_dimension=1, tiled=True
    ).astype(jnp.float32)[:, 0]
    total = lax.psum(shard_sum.astype(jnp.bfloat16), "grp").astype(jnp.float32)
    new_first, new_second = adam_moments(total, moment_first, moment_second)
    correct_first = 1.0 - beta_first**STEP
    correct_second = 1.0 - beta_second**STEP
    direction = (
        new_first / correct_first / (jnp.sqrt(new_second / correct_second) + adam_epsilon)
    ).astype(jnp.bfloat16)
    updates = []
    for matrix in range(7):
        offset = starts[matrix] // n_shard
        run_width = widths[matrix] // n_shard
        direction_now = direction[:, offset : offset + run_width]
        updates.append(
            jnp.dot(basis_of(matrix), direction_now, preferred_element_type=jnp.float32).astype(
                jnp.bfloat16
            )
        )
    return (
        new_first,
        new_second,
        updates[0],
        updates[1],
        updates[2],
        updates[3],
        updates[4],
        updates[5],
        updates[6],
    )


WIDTHS, STARTS = column_runs()
SOURCES = (0, 0, 0, 1, 2, 2)
ORDER = (6, 4, 5, 0, 3, 1, 2)
PIECES = (
    ((4, 0, 896, 0, 0),),
    ((5, 0, 896, 0, 0),),
    ((0, 0, 512, 0, 0), (3, 4096, 384, 512, 0)),
    ((6, 0, 512, 0, 0), (1, 4096, 128, 512, 0), (2, 5120, 128, 640, 0), (3, 6144, 128, 768, 384)),
)
N_SH = 8
N_GR = 4
QCOL = 7168
BCOL = 896
TOK = 128
RANK = 256


def needed_by(matrix):
    return [t for t in range(N_GR) if any(piece[0] == matrix for piece in PIECES[t])]


def gather_reduce(
    acts, hidden, grads, bmain, bdown,
    out_main, out_down, out_g,
    pm, pd, av, hv, gx, pj, term, ybuf, zbuf, gfin,
    lsem, osem, zs, zr, ys, yr, cs, cr, gs, gr, js, jr, rys, ryr, rzs, rzr, fs, fr,
):
    g = lax.axis_index("grp")
    s = lax.axis_index("shard")
    core = g % 2
    cpeer = g + 1 - 2 * core
    ypeer = s + 1 - 2 * (s % 2)

    acts_in = pltpu.make_async_copy(acts, av, lsem.at[0])
    hid_in = pltpu.make_async_copy(hidden, hv, lsem.at[1])
    acts_in.start()
    hid_in.start()
    own_in = []
    for k in range(7):
        if k < 6:
            src = bmain.at[k]
            dst = pm.at[k, pl.ds(pl.multiple_of(s * 512, 512), 512)]
        else:
            src = bdown
            dst = pd.at[pl.ds(pl.multiple_of(s * 896, 128), 896)]
        own_in.append(pltpu.make_async_copy(src, dst, lsem.at[2 + k]))
        own_in[-1].start()

    barrier = pltpu.get_barrier_semaphore()
    for d in range(1, N_GR):
        pl.semaphore_signal(barrier, inc=1, device_id=((g + d) % N_GR, s), device_id_type=MESH)
    for d in range(1, 4):
        pl.semaphore_signal(barrier, inc=1, device_id=(g, (s + 2 * d) % N_SH), device_id_type=MESH)
    pl.semaphore_signal(barrier, inc=1, device_id=(g, ypeer), device_id_type=MESH)
    pl.semaphore_wait(barrier, 7)

    def remote(src, dst, send, recv, grp, shard):
        return pltpu.make_async_remote_copy(
            src_ref=src, dst_ref=dst, send_sem=send, recv_sem=recv,
            device_id=(grp, shard), device_id_type=MESH,
        )

    def full(k, owner, half):
        if k < 6:
            return pm.at[k, pl.ds(pl.multiple_of(owner * 512 + half * 256, 256), 256)]
        return pd.at[pl.ds(pl.multiple_of(owner * 896 + half * 448, 64), 448)]

    def own(k):
        if k < 6:
            return bmain.at[k, pl.ds(pl.multiple_of(core * 256, 256), 256)]
        return bdown.at[pl.ds(pl.multiple_of(core * 448, 64), 448)]

    pending = []
    def send_own(k):
        c = remote(own(k), full(k, s, core), ys.at[k, 0], yr.at[k, 0], g, ypeer)
        c.start()
        pending.append(c)
        for d in (1, 3, 2):
            c = remote(own(k), full(k, s, core), zs.at[k, d - 1], zr.at[k, d - 1], g, (s + 2 * d) % N_SH)
            c.start()
            pending.append(c)

    def send_grads(t):
        for k, base, width, _, first in PIECES[t]:
            if width * N_SH == WIDTHS[k]:
                cuts = [(STARTS[k], base, WIDTHS[k])]
            else:
                run = WIDTHS[k] // N_SH
                cuts = [(STARTS[k] + b * run + first, base + b * width, width) for b in range(N_SH)]
            for a, b, w in cuts:
                @pl.when(g != t)
                def _():
                    remote(
                        grads.at[:, pl.ds(a, w)], gx.at[g, :, pl.ds(b, w)], gs.at[t], gr.at[g], t, s
                    ).start()

                @pl.when(g == t)
                def _():
                    pltpu.make_async_copy(
                        grads.at[:, pl.ds(a, w)], gx.at[t, :, pl.ds(b, w)], gr.at[t]
                    ).start()

    send_own(ORDER[0])
    for t in range(N_GR):
        send_grads(t)
    for k in ORDER[1:]:
        send_own(k)

    def after_z(k):
        for d in (1, 3, 2):
            owner = (s + N_SH - 2 * d) % N_SH
            block = full(k, owner, core)
            remote(block, block, zs.at[k, d - 1], zr.at[k, d - 1], g, ypeer).wait_recv()
            c = remote(block, block, ys.at[k, d], yr.at[k, d], g, ypeer)
            c.start()
            pending.append(c)
            c = remote(block, block, cs.at[k, d - 1], cr.at[k, d - 1], cpeer, s)
            c.start()
            pending.append(c)

    def after_y(k):
        for d in (0, 1, 3, 2):
            owner = (ypeer + N_SH - 2 * d) % N_SH
            block = full(k, owner, core)
            remote(block, block, ys.at[k, d], yr.at[k, d], g, ypeer).wait_recv()
            c = remote(block, block, cs.at[k, 3 + d], cr.at[k, 3 + d], cpeer, s)
            c.start()
            pending.append(c)

    outs = []

    def project(k):
        for d in range(1, 4):
            block = full(k, (s + N_SH - 2 * d) % N_SH, 1 - core)
            remote(block, block, cs.at[k, d - 1], cr.at[k, d - 1], cpeer, s).wait_recv()
        for d in range(4):
            block = full(k, (ypeer + N_SH - 2 * d) % N_SH, 1 - core)
            remote(block, block, cs.at[k, 3 + d], cr.at[k, 3 + d], cpeer, s).wait_recv()
        own_in[k].wait()
        if k < 6:
            c = pltpu.make_async_copy(pm.at[k], out_main.at[k], osem.at[k])
        else:
            c = pltpu.make_async_copy(pd, out_down, osem.at[k])
        c.start()
        outs.append(c)
        x = hv[...] if k == 6 else av[SOURCES[k]]
        p = pd[...] if k == 6 else pm[k]
        pj[k, g] = jnp.dot(x, p, preferred_element_type=jnp.float32).astype(jnp.bfloat16)
        for t in needed_by(k):
            slot = needed_by(k).index(t)

            @pl.when(g != t)
            def _():
                remote(pj.at[k, g], pj.at[k, g], js.at[k, slot], jr.at[k, g], t, s).start()

    acts_waited = False
    for step in range(len(ORDER) + 2):
        if step < len(ORDER):
            after_z(ORDER[step])
        if 1 <= step < len(ORDER) + 1:
            after_y(ORDER[step - 1])
        if step >= 2:
            if not acts_waited:
                acts_in.wait()
                hid_in.wait()
                acts_waited = True
            project(ORDER[step - 2])

    for src in range(N_GR):
        pltpu.make_async_copy(gx.at[src], gx.at[src], gr.at[src]).wait()

    def block_term(t, target):
        for k, base, width, place, _ in PIECES[t]:
            left = pj[k].reshape(N_GR * TOK, RANK)
            cols = pl.ds(pl.multiple_of(base + target * width, 128), width)
            right = gx[:, :, cols].reshape(N_GR * TOK, width)
            value = lax.dot_general(
                left, right, (((0,), (0,)), ((), ())), preferred_element_type=jnp.float32
            )
            term[target, :, place : place + width] = value.astype(jnp.bfloat16)

    for t in range(N_GR):
        @pl.when(g == t)
        def _():
            for k, *_ in PIECES[t]:
                for src in range(N_GR):
                    if src != t:
                        remote(
                            pj.at[k, src], pj.at[k, src], js.at[k, 0], jr.at[k, src], g, ypeer
                        ).wait_recv()

            def far(d, carry):
                target = (ypeer + 2 * d) % N_SH
                block_term(t, target)
                remote(
                    term.at[target], ybuf.at[d % 4], rys.at[d % 4], ryr.at[d % 4], g, ypeer
                ).start()
                return carry

            lax.fori_loop(1, 5, far, 0)

            def near(d, carry):
                block_term(t, (s + 2 * d) % N_SH)
                return carry

            lax.fori_loop(1, 5, near, 0)

    for d in (1, 2, 3, 0):
        target = (s + 2 * d) % N_SH
        remote(ybuf.at[d], ybuf.at[d], rys.at[d], ryr.at[d], g, ypeer).wait_recv()
        total = term[target].astype(jnp.float32) + ybuf[d].astype(jnp.float32)
        if d:
            term[target] = total.astype(jnp.bfloat16)
            c = remote(term.at[target], zbuf.at[d - 1], rzs.at[d - 1], rzr.at[d - 1], g, target)
            c.start()
            pending.append(c)
    for d in (1, 2, 3):
        remote(zbuf.at[d - 1], zbuf.at[d - 1], rzs.at[d - 1], rzr.at[d - 1], g, ypeer).wait_recv()
        total = total + zbuf[d - 1].astype(jnp.float32)
    gfin[...] = total.astype(jnp.bfloat16)
    keep = pltpu.make_async_copy(gfin, out_g.at[g], osem.at[7])
    for d in (2, 3, 1):
        c = remote(gfin, out_g.at[g], fs.at[d - 1], fr.at[d - 1], (g + d) % N_GR, s)
        c.start()
        pending.append(c)
    keep.start()
    for d in (1, 2, 3):
        got = out_g.at[(g + N_GR - d) % N_GR]
        remote(got, got, fs.at[d - 1], fr.at[d - 1], g, ypeer).wait_recv()
    keep.wait()

    for c in pending:
        c.wait_send()
    for d in range(4):
        remote(ybuf.at[d], ybuf.at[d], rys.at[d], ryr.at[d], g, ypeer).wait_send()
    for t in range(N_GR):
        @pl.when(g != t)
        def _():
            remote(gx.at[t], gx.at[t], gs.at[t], gr.at[t], t, s).wait_send()
            for k in range(7):
                if t in needed_by(k):
                    slot = needed_by(k).index(t)
                    remote(pj.at[k, t], pj.at[k, t], js.at[k, slot], jr.at[k, t], t, s).wait_send()
    for c in outs:
        c.wait()


def moments_and_updates(g4, m1, m2, bm, bd, n1, n2, *rest):
    updates, direction = rest[:7], rest[7]

    @pl.when(pl.program_id(0) == 0)
    def _():
        correct_first = 1.0 - beta_first**STEP
        correct_second = 1.0 - beta_second**STEP
        for t in range(N_GR):
            for k, _b, width, place, first in PIECES[t]:
                a = STARTS[k] // N_SH + first
                for c in range(0, width, 128):
                    cols = slice(a + c, a + c + 128)
                    gradient = g4[t, :, place + c : place + c + 128].astype(jnp.float32)
                    new_first, new_second = adam_moments(gradient, m1[:, cols], m2[:, cols])
                    n1[:, cols] = new_first
                    n2[:, cols] = new_second
                    direction[:, cols] = (
                        new_first / correct_first
                        / (jnp.sqrt(new_second / correct_second) + adam_epsilon)
                    ).astype(jnp.bfloat16)

    for k in range(7):
        a = STARTS[k] // N_SH
        w = WIDTHS[k] // N_SH
        basis = bd[...] if k == 6 else bm[k]
        updates[k][...] = jnp.dot(
            basis, direction[:, a : a + w], preferred_element_type=jnp.float32
        ).astype(jnp.bfloat16)


def local_block(acts, hidden, grads, bases_main, bases_down, moment_first, moment_second):
    bf, f32 = jnp.bfloat16, jnp.float32
    anyspace = pl.BlockSpec(memory_space=pl.ANY)
    dma = pltpu.SemaphoreType.DMA
    full_main, full_down, g4 = pl.pallas_call(
        gather_reduce,
        out_shape=(
            jax.ShapeDtypeStruct((6, D, RANK), bf),
            jax.ShapeDtypeStruct((FF, RANK), bf),
            jax.ShapeDtypeStruct((N_GR, RANK, BCOL), bf),
        ),
        in_specs=[anyspace] * 5,
        out_specs=(anyspace,) * 3,
        scratch_shapes=[
            pltpu.VMEM((6, D, RANK), bf),
            pltpu.VMEM((FF, RANK), bf),
            pltpu.VMEM((3, TOK, D), bf),
            pltpu.VMEM((TOK, FF), bf),
            pltpu.VMEM((N_GR, TOK, QCOL), bf),
            pltpu.VMEM((7, N_GR, TOK, RANK), bf),
            pltpu.VMEM((N_SH, RANK, BCOL), bf),
            pltpu.VMEM((4, RANK, BCOL), bf),
            pltpu.VMEM((3, RANK, BCOL), bf),
            pltpu.VMEM((RANK, BCOL), bf),
            dma((9,)), dma((8,)),
            dma((7, 3)), dma((7, 3)), dma((7, 4)), dma((7, 4)), dma((7, 7)), dma((7, 7)),
            dma((4,)), dma((4,)), dma((7, 2)), dma((7, 4)),
            dma((4,)), dma((4,)), dma((3,)), dma((3,)), dma((3,)), dma((3,)),
        ],
        compiler_params=pltpu.CompilerParams(
            collective_id=0, has_side_effects=True, vmem_limit_bytes=56 * 2**20
        ),
    )(acts, hidden, grads, bases_main, bases_down)

    steps = 8
    cols = moment_first.shape[1]
    once = pl.Buffered(1)
    whole = lambda: pl.BlockSpec((RANK, cols), lambda i: (0, 0), pipeline_mode=once)
    runs = [w // N_SH for w in WIDTHS]
    rows = [FF if k == 6 else D for k in range(7)]
    return pl.pallas_call(
        moments_and_updates,
        grid=(steps,),
        out_shape=[jax.ShapeDtypeStruct((RANK, cols), f32)] * 2
        + [jax.ShapeDtypeStruct((rows[k], runs[k]), bf) for k in range(7)],
        in_specs=[
            pl.BlockSpec((N_GR, RANK, BCOL), lambda i: (0, 0, 0), pipeline_mode=once),
            whole(),
            whole(),
            pl.BlockSpec((6, D // steps, RANK), lambda i: (0, i, 0)),
            pl.BlockSpec((FF // steps, RANK), lambda i: (i, 0)),
        ],
        out_specs=[whole(), whole()]
        + [pl.BlockSpec((rows[k] // steps, runs[k]), lambda i: (i, 0)) for k in range(7)],
        scratch_shapes=[pltpu.VMEM((RANK, cols), bf)],
        compiler_params=pltpu.CompilerParams(vmem_limit_bytes=56 * 2**20),
    )(g4, moment_first, moment_second, full_main, full_down)


def solution(mesh):
    block = mesh.shape["grp"] == N_GR and mesh.shape["shard"] == N_SH
    local = local_block if block else local_general
    return jax.shard_map(
        local,
        mesh=mesh,
        in_specs=(
            P(None, ("grp", "shard"), None),
            P(("grp", "shard"), None),
            P(("grp", "shard"), None),
            P(None, "shard", None),
            P("shard", None),
            P(None, "shard"),
            P(None, "shard"),
        ),
        out_specs=(
            P(None, "shard"),
            P(None, "shard"),
            P(None, "shard"),
            P(None, "shard"),
            P(None, "shard"),
            P(None, "shard"),
            P(None, "shard"),
            P(None, "shard"),
            P(None, "shard"),
        ),
        check_vma=False,
    )
```

```python
import functools

import jax
import jax.numpy as jnp
from jax import lax
from jax.experimental import pallas as pl
from jax.experimental.pallas import tpu as pltpu
from jax.sharding import PartitionSpec as P

MESH = pl.DeviceIdType.MESH

D = 4096
KV = 1024
FF = 7168
STEP = 1000


beta_first = 0.9
beta_second = 0.999
adam_epsilon = 1e-08


def column_runs():
    widths = (D, KV, KV, D, FF, FF, D)
    starts = []
    position = 0
    for width in widths:
        starts.append(position)
        position = position + width
    return (widths, starts)


def adam_moments(gradient, first, second):
    updated_first = beta_first * first + (1.0 - beta_first) * gradient
    updated_second = beta_second * second + (1.0 - beta_second) * gradient * gradient
    return (updated_first, updated_second)


def local_general(acts, hidden, grads, bases_main, bases_down, moment_first, moment_second):
    widths, starts = column_runs()
    sources = (0, 0, 0, 1, 2, 2)
    n_shard = lax.axis_size("shard")
    rank = bases_main.shape[2]
    full_main, full_down = (
        lax.all_gather(bases_main, "shard", axis=1, tiled=True),
        lax.all_gather(bases_down[None], "shard", axis=1, tiled=True),
    )
    full_down = full_down[0]

    def basis_of(matrix):
        return full_down if matrix == 6 else full_main[matrix]

    blocks = []
    for matrix in range(7):
        source = hidden if matrix == 6 else acts[sources[matrix]]
        partial_term = jnp.dot(
            jnp.dot(source, basis_of(matrix), preferred_element_type=jnp.float32)
            .astype(jnp.bfloat16)
            .T,
            grads[:, starts[matrix] : starts[matrix] + widths[matrix]],
            preferred_element_type=jnp.float32,
        )
        blocks.append(partial_term.reshape(rank, n_shard, widths[matrix] // n_shard))
    stacked = jnp.concatenate(blocks, axis=2)
    shard_sum = lax.psum_scatter(
        stacked.astype(jnp.bfloat16), "shard", scatter_dimension=1, tiled=True
    ).astype(jnp.float32)[:, 0]
    total = lax.psum(shard_sum.astype(jnp.bfloat16), "grp").astype(jnp.float32)
    new_first, new_second = adam_moments(total, moment_first, moment_second)
    correct_first = 1.0 - beta_first**STEP
    correct_second = 1.0 - beta_second**STEP
    direction = (
        new_first / correct_first / (jnp.sqrt(new_second / correct_second) + adam_epsilon)
    ).astype(jnp.bfloat16)
    updates = []
    for matrix in range(7):
        offset = starts[matrix] // n_shard
        run_width = widths[matrix] // n_shard
        direction_now = direction[:, offset : offset + run_width]
        updates.append(
            jnp.dot(basis_of(matrix), direction_now, preferred_element_type=jnp.float32).astype(
                jnp.bfloat16
            )
        )
    return (
        new_first,
        new_second,
        updates[0],
        updates[1],
        updates[2],
        updates[3],
        updates[4],
        updates[5],
        updates[6],
    )


WIDTHS, STARTS = column_runs()
SOURCES = (0, 0, 0, 1, 2, 2)
ORDER = (6, 4, 5, 0, 3, 1, 2)
PIECES = (
    ((4, 0, 896, 0, 0),),
    ((5, 0, 896, 0, 0),),
    ((0, 0, 512, 0, 0), (3, 4096, 384, 512, 0)),
    ((6, 0, 512, 0, 0), (1, 4096, 128, 512, 0), (2, 5120, 128, 640, 0), (3, 6144, 128, 768, 384)),
)
N_SH = 8
N_GR = 4
QCOL = 7168
BCOL = 896
TOK = 128
RANK = 256


def adam_direction(gradient, first, second):
    new_first, new_second = adam_moments(gradient, first, second)
    correct_first = 1.0 - beta_first**STEP
    correct_second = 1.0 - beta_second**STEP
    direction = (
        new_first / correct_first / (jnp.sqrt(new_second / correct_second) + adam_epsilon)
    ).astype(jnp.bfloat16)
    return new_first, new_second, direction


def needed_by(matrix):
    return [t for t in range(N_GR) if any(piece[0] == matrix for piece in PIECES[t])]


def gather_reduce(
    acts, hidden, grads, bmain, bdown, first, second,
    out_main, out_down, out_g, out_dir,
    pm, pd, av, hv, gx, pj, term, ybuf, zbuf, gall, m1, m2, direction,
    lsem, osem, zs, zr, ys, yr, cs, cr, gs, gr, js, jr, rys, ryr, rzs, rzr, fs, fr,
):
    g = lax.axis_index("grp")
    s = lax.axis_index("shard")
    core = g % 2
    cpeer = g + 1 - 2 * core
    ypeer = s + 1 - 2 * (s % 2)

    acts_in = pltpu.make_async_copy(acts, av, lsem.at[0])
    hid_in = pltpu.make_async_copy(hidden, hv, lsem.at[1])
    acts_in.start()
    hid_in.start()
    first_in = pltpu.make_async_copy(first, m1, lsem.at[9])
    second_in = pltpu.make_async_copy(second, m2, lsem.at[10])
    own_in = []
    for k in range(7):
        if k < 6:
            src = bmain.at[k]
            dst = pm.at[k, pl.ds(pl.multiple_of(s * 512, 512), 512)]
        else:
            src = bdown
            dst = pd.at[pl.ds(pl.multiple_of(s * 896, 128), 896)]
        own_in.append(pltpu.make_async_copy(src, dst, lsem.at[2 + k]))
        own_in[-1].start()

    barrier = pltpu.get_barrier_semaphore()
    for d in range(1, N_GR):
        pl.semaphore_signal(barrier, inc=1, device_id=((g + d) % N_GR, s), device_id_type=MESH)
    for d in range(1, 4):
        pl.semaphore_signal(barrier, inc=1, device_id=(g, (s + 2 * d) % N_SH), device_id_type=MESH)
    pl.semaphore_signal(barrier, inc=1, device_id=(g, ypeer), device_id_type=MESH)
    pl.semaphore_wait(barrier, 7)

    def remote(src, dst, send, recv, grp, shard):
        return pltpu.make_async_remote_copy(
            src_ref=src, dst_ref=dst, send_sem=send, recv_sem=recv,
            device_id=(grp, shard), device_id_type=MESH,
        )

    def full(k, owner, half):
        if k < 6:
            return pm.at[k, pl.ds(pl.multiple_of(owner * 512 + half * 256, 256), 256)]
        return pd.at[pl.ds(pl.multiple_of(owner * 896 + half * 448, 64), 448)]

    def own(k):
        if k < 6:
            return bmain.at[k, pl.ds(pl.multiple_of(core * 256, 256), 256)]
        return bdown.at[pl.ds(pl.multiple_of(core * 448, 64), 448)]

    pending = []
    def send_own(k):
        c = remote(own(k), full(k, s, core), ys.at[k, 0], yr.at[k, 0], g, ypeer)
        c.start()
        pending.append(c)
        for d in (1, 3, 2):
            c = remote(own(k), full(k, s, core), zs.at[k, d - 1], zr.at[k, d - 1], g, (s + 2 * d) % N_SH)
            c.start()
            pending.append(c)

    def send_grads(t):
        for k, base, width, _, first in PIECES[t]:
            if width * N_SH == WIDTHS[k]:
                cuts = [(STARTS[k], base, WIDTHS[k])]
            else:
                run = WIDTHS[k] // N_SH
                cuts = [(STARTS[k] + b * run + first, base + b * width, width) for b in range(N_SH)]
            for a, b, w in cuts:
                @pl.when(g != t)
                def _():
                    remote(
                        grads.at[:, pl.ds(a, w)], gx.at[g, :, pl.ds(b, w)], gs.at[t], gr.at[g], t, s
                    ).start()

                @pl.when(g == t)
                def _():
                    pltpu.make_async_copy(
                        grads.at[:, pl.ds(a, w)], gx.at[t, :, pl.ds(b, w)], gr.at[t]
                    ).start()

    send_own(ORDER[0])
    for t in range(N_GR):
        send_grads(t)
    for k in ORDER[1:]:
        send_own(k)
    first_in.start()
    second_in.start()

    def after_z(k):
        for d in (1, 3, 2):
            owner = (s + N_SH - 2 * d) % N_SH
            block = full(k, owner, core)
            remote(block, block, zs.at[k, d - 1], zr.at[k, d - 1], g, ypeer).wait_recv()
            c = remote(block, block, ys.at[k, d], yr.at[k, d], g, ypeer)
            c.start()
            pending.append(c)
            c = remote(block, block, cs.at[k, d - 1], cr.at[k, d - 1], cpeer, s)
            c.start()
            pending.append(c)

    def after_y(k):
        for d in (0, 1, 3, 2):
            owner = (ypeer + N_SH - 2 * d) % N_SH
            block = full(k, owner, core)
            remote(block, block, ys.at[k, d], yr.at[k, d], g, ypeer).wait_recv()
            c = remote(block, block, cs.at[k, 3 + d], cr.at[k, 3 + d], cpeer, s)
            c.start()
            pending.append(c)

    outs = []

    def project(k):
        for d in range(1, 4):
            block = full(k, (s + N_SH - 2 * d) % N_SH, 1 - core)
            remote(block, block, cs.at[k, d - 1], cr.at[k, d - 1], cpeer, s).wait_recv()
        for d in range(4):
            block = full(k, (ypeer + N_SH - 2 * d) % N_SH, 1 - core)
            remote(block, block, cs.at[k, 3 + d], cr.at[k, 3 + d], cpeer, s).wait_recv()
        own_in[k].wait()
        if k < 6:
            c = pltpu.make_async_copy(pm.at[k], out_main.at[k], osem.at[k])
        else:
            c = pltpu.make_async_copy(pd, out_down, osem.at[k])
        c.start()
        outs.append(c)
        x = hv[...] if k == 6 else av[SOURCES[k]]
        p = pd[...] if k == 6 else pm[k]
        pj[k, g] = jnp.dot(x, p, preferred_element_type=jnp.float32).astype(jnp.bfloat16)
        for t in needed_by(k):
            slot = needed_by(k).index(t)

            @pl.when(g != t)
            def _():
                remote(pj.at[k, g], pj.at[k, g], js.at[k, slot], jr.at[k, g], t, s).start()

    acts_waited = False
    for step in range(len(ORDER) + 2):
        if step < len(ORDER):
            after_z(ORDER[step])
        if 1 <= step < len(ORDER) + 1:
            after_y(ORDER[step - 1])
        if step >= 2:
            if not acts_waited:
                acts_in.wait()
                hid_in.wait()
                acts_waited = True
            project(ORDER[step - 2])

    for src in range(N_GR):
        pltpu.make_async_copy(gx.at[src], gx.at[src], gr.at[src]).wait()

    def block_term(t, target):
        for k, base, width, place, _ in PIECES[t]:
            left = pj[k].reshape(N_GR * TOK, RANK)
            cols = pl.ds(pl.multiple_of(base + target * width, 128), width)
            right = gx[:, :, cols].reshape(N_GR * TOK, width)
            value = lax.dot_general(
                left, right, (((0,), (0,)), ((), ())), preferred_element_type=jnp.float32
            )
            term[target, :, place : place + width] = value.astype(jnp.bfloat16)

    for t in range(N_GR):
        @pl.when(g == t)
        def _():
            for k, *_ in PIECES[t]:
                for src in range(N_GR):
                    if src != t:
                        remote(
                            pj.at[k, src], pj.at[k, src], js.at[k, 0], jr.at[k, src], g, ypeer
                        ).wait_recv()

            def far(d, carry):
                target = (ypeer + 2 * d) % N_SH
                block_term(t, target)
                remote(
                    term.at[target], ybuf.at[d % 4], rys.at[d % 4], ryr.at[d % 4], g, ypeer
                ).start()
                return carry

            lax.fori_loop(1, 5, far, 0)

            def near(d, carry):
                block_term(t, (s + 2 * d) % N_SH)
                return carry

            lax.fori_loop(1, 5, near, 0)

    for d in (1, 2, 3, 0):
        target = (s + 2 * d) % N_SH
        remote(ybuf.at[d], ybuf.at[d], rys.at[d], ryr.at[d], g, ypeer).wait_recv()
        total = term[target].astype(jnp.float32) + ybuf[d].astype(jnp.float32)
        if d:
            term[target] = total.astype(jnp.bfloat16)
            c = remote(term.at[target], zbuf.at[d - 1], rzs.at[d - 1], rzr.at[d - 1], g, target)
            c.start()
            pending.append(c)
    for d in (1, 2, 3):
        remote(zbuf.at[d - 1], zbuf.at[d - 1], rzs.at[d - 1], rzr.at[d - 1], g, ypeer).wait_recv()
        total = total + zbuf[d - 1].astype(jnp.float32)
    gall[g] = total.astype(jnp.bfloat16)
    across = (g + 2) % N_GR
    diagonal = (cpeer + 2) % N_GR
    c = remote(gall.at[g], gall.at[g], fs.at[0], fr.at[0], across, s)
    c.start()
    pending.append(c)
    c = remote(gall.at[g], gall.at[g], fs.at[1], fr.at[1], cpeer, s)
    c.start()
    pending.append(c)
    first_in.wait()
    second_in.wait()

    def direct(quarter):
        for t in range(N_GR):
            @pl.when(quarter == t)
            def _():
                def chunk(c, carry):
                    if t == 2:
                        col = 128 * c + 256 * (c // 4)
                    elif t == 3:
                        late = c // 4
                        col = (1 - late) * (3072 + 128 * c) + late * (128 * c + 384 * (c // 6))
                    else:
                        col = 1280 + BCOL * t + 128 * c
                    cols = pl.ds(pl.multiple_of(col, 128), 128)
                    gradient = gall[t, :, pl.ds(pl.multiple_of(128 * c, 128), 128)]
                    _, _, value = adam_direction(
                        gradient.astype(jnp.float32), m1[:, cols], m2[:, cols]
                    )
                    direction[:, cols] = value
                    return carry

                lax.fori_loop(0, BCOL // 128, chunk, 0)

    direct(g)
    remote(gall.at[cpeer], gall.at[cpeer], fs.at[1], fr.at[1], cpeer, s).wait_recv()
    direct(cpeer)
    remote(gall.at[across], gall.at[across], fs.at[0], fr.at[0], across, s).wait_recv()
    c = remote(gall.at[across], gall.at[across], fs.at[2], fr.at[2], cpeer, s)
    c.start()
    pending.append(c)
    direct(across)
    remote(gall.at[diagonal], gall.at[diagonal], fs.at[2], fr.at[2], cpeer, s).wait_recv()
    keep = pltpu.make_async_copy(gall, out_g, osem.at[7])
    keep.start()
    outs.append(keep)
    direct(diagonal)
    keep = pltpu.make_async_copy(direction, out_dir, osem.at[8])
    keep.start()
    outs.append(keep)

    for c in pending:
        c.wait_send()
    for d in range(4):
        remote(ybuf.at[d], ybuf.at[d], rys.at[d], ryr.at[d], g, ypeer).wait_send()
    for t in range(N_GR):
        @pl.when(g != t)
        def _():
            remote(gx.at[t], gx.at[t], gs.at[t], gr.at[t], t, s).wait_send()
            for k in range(7):
                if t in needed_by(k):
                    slot = needed_by(k).index(t)
                    remote(pj.at[k, t], pj.at[k, t], js.at[k, slot], jr.at[k, t], t, s).wait_send()
    for c in outs:
        c.wait()


def moments_and_updates(g4, m1, m2, direction, bm, bd, n1, n2, *updates):
    for t in range(N_GR):
        for k, _b, width, place, first in PIECES[t]:
            cols = slice(STARTS[k] // N_SH + first, STARTS[k] // N_SH + first + width)
            gradient = g4[t, :, place : place + width].astype(jnp.float32)
            n1[:, cols], n2[:, cols] = adam_moments(gradient, m1[:, cols], m2[:, cols])

    for k in range(7):
        a = STARTS[k] // N_SH
        w = WIDTHS[k] // N_SH
        basis = bd[...] if k == 6 else bm[k]
        updates[k][...] = jnp.dot(
            basis, direction[:, a : a + w], preferred_element_type=jnp.float32
        ).astype(jnp.bfloat16)


def local_block(acts, hidden, grads, bases_main, bases_down, moment_first, moment_second):
    bf, f32 = jnp.bfloat16, jnp.float32
    anyspace = pl.BlockSpec(memory_space=pl.ANY)
    dma = pltpu.SemaphoreType.DMA
    full_main, full_down, g4, direction = pl.pallas_call(
        gather_reduce,
        out_shape=(
            jax.ShapeDtypeStruct((6, D, RANK), bf),
            jax.ShapeDtypeStruct((FF, RANK), bf),
            jax.ShapeDtypeStruct((N_GR, RANK, BCOL), bf),
            jax.ShapeDtypeStruct((RANK, moment_first.shape[1]), bf),
        ),
        in_specs=[anyspace] * 7,
        out_specs=(anyspace,) * 4,
        scratch_shapes=[
            pltpu.VMEM((6, D, RANK), bf),
            pltpu.VMEM((FF, RANK), bf),
            pltpu.VMEM((3, TOK, D), bf),
            pltpu.VMEM((TOK, FF), bf),
            pltpu.VMEM((N_GR, TOK, QCOL), bf),
            pltpu.VMEM((7, N_GR, TOK, RANK), bf),
            pltpu.VMEM((N_SH, RANK, BCOL), bf),
            pltpu.VMEM((4, RANK, BCOL), bf),
            pltpu.VMEM((3, RANK, BCOL), bf),
            pltpu.VMEM((N_GR, RANK, BCOL), bf),
            pltpu.VMEM(moment_first.shape, f32),
            pltpu.VMEM(moment_first.shape, f32),
            pltpu.VMEM(moment_first.shape, bf),
            dma((11,)), dma((9,)),
            dma((7, 3)), dma((7, 3)), dma((7, 4)), dma((7, 4)), dma((7, 7)), dma((7, 7)),
            dma((4,)), dma((4,)), dma((7, 2)), dma((7, 4)),
            dma((4,)), dma((4,)), dma((3,)), dma((3,)), dma((3,)), dma((3,)),
        ],
        compiler_params=pltpu.CompilerParams(
            collective_id=0, has_side_effects=True, vmem_limit_bytes=56 * 2**20
        ),
    )(acts, hidden, grads, bases_main, bases_down, moment_first, moment_second)

    steps = 8
    cols = moment_first.shape[1]
    once = pl.Buffered(1)
    band = lambda: pl.BlockSpec((RANK // steps, cols), lambda i: (i, 0))
    runs = [w // N_SH for w in WIDTHS]
    rows = [FF if k == 6 else D for k in range(7)]
    return pl.pallas_call(
        moments_and_updates,
        grid=(steps,),
        out_shape=[jax.ShapeDtypeStruct((RANK, cols), f32)] * 2
        + [jax.ShapeDtypeStruct((rows[k], runs[k]), bf) for k in range(7)],
        in_specs=[
            pl.BlockSpec((N_GR, RANK // steps, BCOL), lambda i: (0, i, 0)),
            band(),
            band(),
            pl.BlockSpec((RANK, cols), lambda i: (0, 0), pipeline_mode=once),
            pl.BlockSpec((6, D // steps, RANK), lambda i: (0, i, 0)),
            pl.BlockSpec((FF // steps, RANK), lambda i: (i, 0)),
        ],
        out_specs=[band(), band()]
        + [pl.BlockSpec((rows[k] // steps, runs[k]), lambda i: (i, 0)) for k in range(7)],
        compiler_params=pltpu.CompilerParams(vmem_limit_bytes=56 * 2**20),
    )(g4, moment_first, moment_second, direction, full_main, full_down)


def solution(mesh):
    block = mesh.shape["grp"] == N_GR and mesh.shape["shard"] == N_SH
    local = local_block if block else local_general
    return jax.shard_map(
        local,
        mesh=mesh,
        in_specs=(
            P(None, ("grp", "shard"), None),
            P(("grp", "shard"), None),
            P(("grp", "shard"), None),
            P(None, "shard", None),
            P("shard", None),
            P(None, "shard"),
            P(None, "shard"),
        ),
        out_specs=(
            P(None, "shard"),
            P(None, "shard"),
            P(None, "shard"),
            P(None, "shard"),
            P(None, "shard"),
            P(None, "shard"),
            P(None, "shard"),
            P(None, "shard"),
            P(None, "shard"),
        ),
        check_vma=False,
    )
```

```python
import functools

import jax
import jax.numpy as jnp
from jax import lax
from jax.experimental import pallas as pl
from jax.experimental.pallas import tpu as pltpu
from jax.sharding import PartitionSpec as P

MESH = pl.DeviceIdType.MESH

D = 4096
KV = 1024
FF = 7168
STEP = 1000


beta_first = 0.9
beta_second = 0.999
adam_epsilon = 1e-08


def column_runs():
    widths = (D, KV, KV, D, FF, FF, D)
    starts = []
    position = 0
    for width in widths:
        starts.append(position)
        position = position + width
    return (widths, starts)


def adam_moments(gradient, first, second):
    updated_first = beta_first * first + (1.0 - beta_first) * gradient
    updated_second = beta_second * second + (1.0 - beta_second) * gradient * gradient
    return (updated_first, updated_second)


def local_general(acts, hidden, grads, bases_main, bases_down, moment_first, moment_second):
    widths, starts = column_runs()
    sources = (0, 0, 0, 1, 2, 2)
    n_shard = lax.axis_size("shard")
    rank = bases_main.shape[2]
    full_main, full_down = (
        lax.all_gather(bases_main, "shard", axis=1, tiled=True),
        lax.all_gather(bases_down[None], "shard", axis=1, tiled=True),
    )
    full_down = full_down[0]

    def basis_of(matrix):
        return full_down if matrix == 6 else full_main[matrix]

    blocks = []
    for matrix in range(7):
        source = hidden if matrix == 6 else acts[sources[matrix]]
        partial_term = jnp.dot(
            jnp.dot(source, basis_of(matrix), preferred_element_type=jnp.float32)
            .astype(jnp.bfloat16)
            .T,
            grads[:, starts[matrix] : starts[matrix] + widths[matrix]],
            preferred_element_type=jnp.float32,
        )
        blocks.append(partial_term.reshape(rank, n_shard, widths[matrix] // n_shard))
    stacked = jnp.concatenate(blocks, axis=2)
    shard_sum = lax.psum_scatter(
        stacked.astype(jnp.bfloat16), "shard", scatter_dimension=1, tiled=True
    ).astype(jnp.float32)[:, 0]
    total = lax.psum(shard_sum.astype(jnp.bfloat16), "grp").astype(jnp.float32)
    new_first, new_second = adam_moments(total, moment_first, moment_second)
    correct_first = 1.0 - beta_first**STEP
    correct_second = 1.0 - beta_second**STEP
    direction = (
        new_first / correct_first / (jnp.sqrt(new_second / correct_second) + adam_epsilon)
    ).astype(jnp.bfloat16)
    updates = []
    for matrix in range(7):
        offset = starts[matrix] // n_shard
        run_width = widths[matrix] // n_shard
        direction_now = direction[:, offset : offset + run_width]
        updates.append(
            jnp.dot(basis_of(matrix), direction_now, preferred_element_type=jnp.float32).astype(
                jnp.bfloat16
            )
        )
    return (
        new_first,
        new_second,
        updates[0],
        updates[1],
        updates[2],
        updates[3],
        updates[4],
        updates[5],
        updates[6],
    )


WIDTHS, STARTS = column_runs()
SOURCES = (0, 0, 0, 1, 2, 2)
ORDER = (6, 4, 5, 0, 3, 1, 2)
PIECES = (
    ((4, 0, 896, 0, 0),),
    ((5, 0, 896, 0, 0),),
    ((0, 0, 512, 0, 0), (3, 4096, 384, 512, 0)),
    ((6, 0, 512, 0, 0), (1, 4096, 128, 512, 0), (2, 5120, 128, 640, 0), (3, 6144, 128, 768, 384)),
)
N_SH = 8
N_GR = 4
QCOL = 7168
BCOL = 896
TOK = 128
RANK = 256


def adam_direction(gradient, first, second):
    new_first, new_second = adam_moments(gradient, first, second)
    correct_first = 1.0 - beta_first**STEP
    correct_second = 1.0 - beta_second**STEP
    direction = (
        new_first / correct_first / (jnp.sqrt(new_second / correct_second) + adam_epsilon)
    ).astype(jnp.bfloat16)
    return new_first, new_second, direction


def needed_by(matrix):
    return [t for t in range(N_GR) if any(piece[0] == matrix for piece in PIECES[t])]


def gather_reduce(
    acts, hidden, grads, bmain, bdown, first, second,
    out_main, out_down, out_g, out_dir,
    pm, pd, av, hv, gx, pj, term, ybuf, zbuf, gall, m1, m2, direction,
    lsem, osem, zs, zr, ys, yr, cs, cr, gs, gr, js, jr, rys, ryr, rzs, rzr, fs, fr,
):
    g = lax.axis_index("grp")
    s = lax.axis_index("shard")
    core = g % 2
    cpeer = g + 1 - 2 * core
    ypeer = s + 1 - 2 * (s % 2)

    acts_in = pltpu.make_async_copy(acts, av, lsem.at[0])
    hid_in = pltpu.make_async_copy(hidden, hv, lsem.at[1])
    acts_in.start()
    hid_in.start()
    first_in = pltpu.make_async_copy(first, m1, lsem.at[9])
    second_in = pltpu.make_async_copy(second, m2, lsem.at[10])
    own_in = []
    for k in range(7):
        if k < 6:
            src = bmain.at[k]
            dst = pm.at[k, pl.ds(pl.multiple_of(s * 512, 512), 512)]
        else:
            src = bdown
            dst = pd.at[pl.ds(pl.multiple_of(s * 896, 128), 896)]
        own_in.append(pltpu.make_async_copy(src, dst, lsem.at[2 + k]))
        own_in[-1].start()

    barrier = pltpu.get_barrier_semaphore()
    for d in range(1, N_GR):
        pl.semaphore_signal(barrier, inc=1, device_id=((g + d) % N_GR, s), device_id_type=MESH)
    for d in range(1, 4):
        pl.semaphore_signal(barrier, inc=1, device_id=(g, (s + 2 * d) % N_SH), device_id_type=MESH)
    pl.semaphore_signal(barrier, inc=1, device_id=(g, ypeer), device_id_type=MESH)
    pl.semaphore_wait(barrier, 7)

    def remote(src, dst, send, recv, grp, shard):
        return pltpu.make_async_remote_copy(
            src_ref=src, dst_ref=dst, send_sem=send, recv_sem=recv,
            device_id=(grp, shard), device_id_type=MESH,
        )

    def full(k, owner, half):
        if k < 6:
            return pm.at[k, pl.ds(pl.multiple_of(owner * 512 + half * 256, 256), 256)]
        return pd.at[pl.ds(pl.multiple_of(owner * 896 + half * 448, 64), 448)]

    def own(k):
        if k < 6:
            return bmain.at[k, pl.ds(pl.multiple_of(core * 256, 256), 256)]
        return bdown.at[pl.ds(pl.multiple_of(core * 448, 64), 448)]

    pending = []
    def send_own(k):
        c = remote(own(k), full(k, s, core), ys.at[k, 0], yr.at[k, 0], g, ypeer)
        c.start()
        pending.append(c)
        for d in (1, 3, 2):
            c = remote(own(k), full(k, s, core), zs.at[k, d - 1], zr.at[k, d - 1], g, (s + 2 * d) % N_SH)
            c.start()
            pending.append(c)

    def send_grads(t):
        for k, base, width, _, first in PIECES[t]:
            if width * N_SH == WIDTHS[k]:
                cuts = [(STARTS[k], base, WIDTHS[k])]
            else:
                run = WIDTHS[k] // N_SH
                cuts = [(STARTS[k] + b * run + first, base + b * width, width) for b in range(N_SH)]
            for a, b, w in cuts:
                @pl.when(g != t)
                def _():
                    remote(
                        grads.at[:, pl.ds(a, w)], gx.at[g, :, pl.ds(b, w)], gs.at[t], gr.at[g], t, s
                    ).start()

                @pl.when(g == t)
                def _():
                    pltpu.make_async_copy(
                        grads.at[:, pl.ds(a, w)], gx.at[t, :, pl.ds(b, w)], gr.at[t]
                    ).start()

    send_own(ORDER[0])
    for t in range(N_GR):
        send_grads(t)
    for k in ORDER[1:]:
        send_own(k)
    first_in.start()
    second_in.start()

    def after_z(k):
        for d in (1, 3, 2):
            owner = (s + N_SH - 2 * d) % N_SH
            block = full(k, owner, core)
            remote(block, block, zs.at[k, d - 1], zr.at[k, d - 1], g, ypeer).wait_recv()
            c = remote(block, block, ys.at[k, d], yr.at[k, d], g, ypeer)
            c.start()
            pending.append(c)
            c = remote(block, block, cs.at[k, d - 1], cr.at[k, d - 1], cpeer, s)
            c.start()
            pending.append(c)

    def after_y(k):
        for d in (0, 1, 3, 2):
            owner = (ypeer + N_SH - 2 * d) % N_SH
            block = full(k, owner, core)
            remote(block, block, ys.at[k, d], yr.at[k, d], g, ypeer).wait_recv()
            c = remote(block, block, cs.at[k, 3 + d], cr.at[k, 3 + d], cpeer, s)
            c.start()
            pending.append(c)

    outs = []

    def project(k):
        for d in range(1, 4):
            block = full(k, (s + N_SH - 2 * d) % N_SH, 1 - core)
            remote(block, block, cs.at[k, d - 1], cr.at[k, d - 1], cpeer, s).wait_recv()
        for d in range(4):
            block = full(k, (ypeer + N_SH - 2 * d) % N_SH, 1 - core)
            remote(block, block, cs.at[k, 3 + d], cr.at[k, 3 + d], cpeer, s).wait_recv()
        own_in[k].wait()
        if k < 6:
            c = pltpu.make_async_copy(pm.at[k], out_main.at[k], osem.at[k])
        else:
            c = pltpu.make_async_copy(pd, out_down, osem.at[k])
        c.start()
        outs.append(c)
        x = hv[...] if k == 6 else av[SOURCES[k]]
        p = pd[...] if k == 6 else pm[k]
        pj[k, g] = jnp.dot(x, p, preferred_element_type=jnp.float32).astype(jnp.bfloat16)
        for t in needed_by(k):
            slot = needed_by(k).index(t)

            @pl.when(g != t)
            def _():
                remote(pj.at[k, g], pj.at[k, g], js.at[k, slot], jr.at[k, g], t, s).start()

    acts_waited = False
    for step in range(len(ORDER) + 2):
        if step < len(ORDER):
            after_z(ORDER[step])
        if 1 <= step < len(ORDER) + 1:
            after_y(ORDER[step - 1])
        if step >= 2:
            if not acts_waited:
                acts_in.wait()
                hid_in.wait()
                acts_waited = True
            project(ORDER[step - 2])

    for src in range(N_GR):
        pltpu.make_async_copy(gx.at[src], gx.at[src], gr.at[src]).wait()

    def block_term(t, target):
        for k, base, width, place, _ in PIECES[t]:
            left = pj[k].reshape(N_GR * TOK, RANK)
            cols = pl.ds(pl.multiple_of(base + target * width, 128), width)
            right = gx[:, :, cols].reshape(N_GR * TOK, width)
            value = lax.dot_general(
                left, right, (((0,), (0,)), ((), ())), preferred_element_type=jnp.float32
            )
            term[target, :, place : place + width] = value.astype(jnp.bfloat16)

    for t in range(N_GR):
        @pl.when(g == t)
        def _():
            for k, *_ in PIECES[t]:
                for src in range(N_GR):
                    if src != t:
                        remote(
                            pj.at[k, src], pj.at[k, src], js.at[k, 0], jr.at[k, src], g, ypeer
                        ).wait_recv()

            def far(d, carry):
                target = (ypeer + 2 * d) % N_SH
                block_term(t, target)
                remote(
                    term.at[target], ybuf.at[d % 4], rys.at[d % 4], ryr.at[d % 4], g, ypeer
                ).start()
                return carry

            lax.fori_loop(1, 5, far, 0)

            def near(d, carry):
                block_term(t, (s + 2 * d) % N_SH)
                return carry

            lax.fori_loop(1, 5, near, 0)

    for d in (1, 2, 3, 0):
        target = (s + 2 * d) % N_SH
        remote(ybuf.at[d], ybuf.at[d], rys.at[d], ryr.at[d], g, ypeer).wait_recv()
        total = term[target].astype(jnp.float32) + ybuf[d].astype(jnp.float32)
        if d:
            term[target] = total.astype(jnp.bfloat16)
            c = remote(term.at[target], zbuf.at[d - 1], rzs.at[d - 1], rzr.at[d - 1], g, target)
            c.start()
            pending.append(c)
    for d in (1, 2, 3):
        remote(zbuf.at[d - 1], zbuf.at[d - 1], rzs.at[d - 1], rzr.at[d - 1], g, ypeer).wait_recv()
        total = total + zbuf[d - 1].astype(jnp.float32)
    gall[g] = total.astype(jnp.bfloat16)
    across = (g + 2) % N_GR
    diagonal = (cpeer + 2) % N_GR
    c = remote(gall.at[g], gall.at[g], fs.at[0], fr.at[0], across, s)
    c.start()
    pending.append(c)
    c = remote(gall.at[g], gall.at[g], fs.at[1], fr.at[1], cpeer, s)
    c.start()
    pending.append(c)
    first_in.wait()
    second_in.wait()

    def direct(quarter):
        for t in range(N_GR):
            @pl.when(quarter == t)
            def _():
                def chunk(c, carry):
                    if t == 2:
                        col = 128 * c + 256 * (c // 4)
                    elif t == 3:
                        late = c // 4
                        col = (1 - late) * (3072 + 128 * c) + late * (128 * c + 384 * (c // 6))
                    else:
                        col = 1280 + BCOL * t + 128 * c
                    cols = pl.ds(pl.multiple_of(col, 128), 128)
                    gradient = gall[t, :, pl.ds(pl.multiple_of(128 * c, 128), 128)]
                    _, _, value = adam_direction(
                        gradient.astype(jnp.float32), m1[:, cols], m2[:, cols]
                    )
                    direction[:, cols] = value
                    return carry

                lax.fori_loop(0, BCOL // 128, chunk, 0)

    direct(g)
    remote(gall.at[cpeer], gall.at[cpeer], fs.at[1], fr.at[1], cpeer, s).wait_recv()
    direct(cpeer)
    remote(gall.at[across], gall.at[across], fs.at[0], fr.at[0], across, s).wait_recv()
    c = remote(gall.at[across], gall.at[across], fs.at[2], fr.at[2], cpeer, s)
    c.start()
    pending.append(c)
    direct(across)
    remote(gall.at[diagonal], gall.at[diagonal], fs.at[2], fr.at[2], cpeer, s).wait_recv()
    keep = pltpu.make_async_copy(gall, out_g, osem.at[7])
    keep.start()
    outs.append(keep)
    direct(diagonal)
    keep = pltpu.make_async_copy(direction, out_dir, osem.at[8])
    keep.start()
    outs.append(keep)

    for c in pending:
        c.wait_send()
    for d in range(4):
        remote(ybuf.at[d], ybuf.at[d], rys.at[d], ryr.at[d], g, ypeer).wait_send()
    for t in range(N_GR):
        @pl.when(g != t)
        def _():
            remote(gx.at[t], gx.at[t], gs.at[t], gr.at[t], t, s).wait_send()
            for k in range(7):
                if t in needed_by(k):
                    slot = needed_by(k).index(t)
                    remote(pj.at[k, t], pj.at[k, t], js.at[k, slot], jr.at[k, t], t, s).wait_send()
    for c in outs:
        c.wait()


def moments_and_updates(g4, m1, m2, direction, bm, bd, n1, n2, *updates):
    for t in range(N_GR):
        for k, _b, width, place, first in PIECES[t]:
            cols = slice(STARTS[k] // N_SH + first, STARTS[k] // N_SH + first + width)
            gradient = g4[t, :, place : place + width].astype(jnp.float32)
            n1[:, cols], n2[:, cols] = adam_moments(gradient, m1[:, cols], m2[:, cols])

    for k in range(7):
        a = STARTS[k] // N_SH
        w = WIDTHS[k] // N_SH
        basis = bd[...] if k == 6 else bm[k]
        updates[k][...] = jnp.dot(
            basis, direction[:, a : a + w], preferred_element_type=jnp.float32
        ).astype(jnp.bfloat16)


def local_block(acts, hidden, grads, bases_main, bases_down, moment_first, moment_second):
    bf, f32 = jnp.bfloat16, jnp.float32
    anyspace = pl.BlockSpec(memory_space=pl.ANY)
    dma = pltpu.SemaphoreType.DMA
    full_main, full_down, g4, direction = pl.pallas_call(
        gather_reduce,
        out_shape=(
            jax.ShapeDtypeStruct((6, D, RANK), bf),
            jax.ShapeDtypeStruct((FF, RANK), bf),
            jax.ShapeDtypeStruct((N_GR, RANK, BCOL), bf),
            jax.ShapeDtypeStruct((RANK, moment_first.shape[1]), bf),
        ),
        in_specs=[anyspace] * 7,
        out_specs=(anyspace,) * 4,
        scratch_shapes=[
            pltpu.VMEM((6, D, RANK), bf),
            pltpu.VMEM((FF, RANK), bf),
            pltpu.VMEM((3, TOK, D), bf),
            pltpu.VMEM((TOK, FF), bf),
            pltpu.VMEM((N_GR, TOK, QCOL), bf),
            pltpu.VMEM((7, N_GR, TOK, RANK), bf),
            pltpu.VMEM((N_SH, RANK, BCOL), bf),
            pltpu.VMEM((4, RANK, BCOL), bf),
            pltpu.VMEM((3, RANK, BCOL), bf),
            pltpu.VMEM((N_GR, RANK, BCOL), bf),
            pltpu.VMEM(moment_first.shape, f32),
            pltpu.VMEM(moment_first.shape, f32),
            pltpu.VMEM(moment_first.shape, bf),
            dma((11,)), dma((9,)),
            dma((7, 3)), dma((7, 3)), dma((7, 4)), dma((7, 4)), dma((7, 7)), dma((7, 7)),
            dma((4,)), dma((4,)), dma((7, 2)), dma((7, 4)),
            dma((4,)), dma((4,)), dma((3,)), dma((3,)), dma((3,)), dma((3,)),
        ],
        compiler_params=pltpu.CompilerParams(
            collective_id=0, has_side_effects=True, vmem_limit_bytes=56 * 2**20
        ),
    )(acts, hidden, grads, bases_main, bases_down, moment_first, moment_second)

    steps = 4
    cols = moment_first.shape[1]
    once = pl.Buffered(1)
    band = lambda: pl.BlockSpec((RANK // steps, cols), lambda i: (i, 0))
    runs = [w // N_SH for w in WIDTHS]
    rows = [FF if k == 6 else D for k in range(7)]
    return pl.pallas_call(
        moments_and_updates,
        grid=(steps,),
        out_shape=[jax.ShapeDtypeStruct((RANK, cols), f32)] * 2
        + [jax.ShapeDtypeStruct((rows[k], runs[k]), bf) for k in range(7)],
        in_specs=[
            pl.BlockSpec((N_GR, RANK // steps, BCOL), lambda i: (0, i, 0)),
            band(),
            band(),
            pl.BlockSpec((RANK, cols), lambda i: (0, 0), pipeline_mode=once),
            pl.BlockSpec((6, D // steps, RANK), lambda i: (0, i, 0)),
            pl.BlockSpec((FF // steps, RANK), lambda i: (i, 0)),
        ],
        out_specs=[band(), band()]
        + [pl.BlockSpec((rows[k] // steps, runs[k]), lambda i: (i, 0)) for k in range(7)],
        compiler_params=pltpu.CompilerParams(vmem_limit_bytes=56 * 2**20),
    )(g4, moment_first, moment_second, direction, full_main, full_down)


def solution(mesh):
    block = mesh.shape["grp"] == N_GR and mesh.shape["shard"] == N_SH
    local = local_block if block else local_general
    return jax.shard_map(
        local,
        mesh=mesh,
        in_specs=(
            P(None, ("grp", "shard"), None),
            P(("grp", "shard"), None),
            P(("grp", "shard"), None),
            P(None, "shard", None),
            P("shard", None),
            P(None, "shard"),
            P(None, "shard"),
        ),
        out_specs=(
            P(None, "shard"),
            P(None, "shard"),
            P(None, "shard"),
            P(None, "shard"),
            P(None, "shard"),
            P(None, "shard"),
            P(None, "shard"),
            P(None, "shard"),
            P(None, "shard"),
        ),
        check_vma=False,
    )
```
